32 devices in a mesh: expert: 8 (over z, y), dp: 4 (over x, core).
Axes of the slice: x: 2, y: 2, z: 4, core: 2. Of those that a mesh axis runs over, the one named last changes fastest.
Arguments:
- tokens: bfloat16 [4096, 3584], P(('expert', 'dp')), may hold values from -6 to 6
- cotangent: bfloat16 [4096, 3584], P(('expert', 'dp')), may hold values from -6 to 6
- routes: int32 [4096, 2], P(('expert', 'dp')), may hold values from 0 to 7, all different within a row; in each aligned block of 128 rows (0 to 127, 128 to 255, ...) at most 36 rows name the same one
- combine_weights: float32 [4096, 2], P(('expert', 'dp')), may hold values from 0.1 to 1
- gate_weight: bfloat16 [8, 3584, 1024], P('expert', 'dp'), may hold values from -0.09375 to 0.09375
- up_weight: bfloat16 [8, 3584, 1024], P('expert', 'dp'), may hold values from -0.09375 to 0.09375
- down_weight_t: bfloat16 [8, 3584, 1024], P('expert', 'dp'), may hold values from -0.1875 to 0.1875
- sketch_bucket: int32 [3584], replicated, may hold values from 0 to 127
- sketch_sign: int32 [3584], replicated, may hold values 0 or 1
- error_state: float32 [8, 4, 3, 128, 1024], P('expert', 'dp'), may hold values from -4 to 4
Outputs:
- layer_out: bfloat16 [4096, 3584], P(('expert', 'dp'))
- input_grad: bfloat16 [4096, 3584], P(('expert', 'dp'))
- sketch_total: float32 [8, 3, 128, 1024], P('expert')
- error_next: float32 [8, 4, 3, 128, 1024], P('expert', 'dp')
The draws below stay inside these ranges and needn't reach their ends.
Inputs may be any that keep to these rules, and one draw needn't show every extreme that they name: `routes`: each token names 2 different experts; the rows of one device name one expert at most 36 times, and in every draw the rows of some device name some expert exactly 36 times.
All inputs are finite; a program needn't handle non-finite values.
Results may differ from the reference program's by a relative error of at most 0.0065.
Values may be sent and summed in bfloat16 or wider, within the bound.
A program may use at most 128 MiB of HBM per device.

```python
import math
import jax
import jax.numpy as jnp
import numpy as np
from jax import lax

D = 3584
H = 1024
TOP = 2
SKETCH = 128
TOK_DEV = 128
EXPERTS = 8
CAP = 36
TOKENS = 4096
N_EXPERT = 8
N_DP = 4


def touch_ends(array, stream_key, least, largest):
    place = [jax.random.randint(jax.random.fold_in(stream_key, axis), (), 0, length) for axis, length in enumerate(array.shape)]
    widest = array.shape.index(max(array.shape))
    beside = place[:widest] + [(place[widest] + 1) % array.shape[widest]] + place[widest + 1:]
    return array.at[tuple(place)].set(least).at[tuple(beside)].set(largest)


def level_of(key, shape, pieces, least, high):
    def one(axis_at, parts):
        steps = jax.random.uniform(jax.random.fold_in(jax.random.fold_in(key, 6), axis_at), (parts,), jnp.float32, least / len(pieces), high / len(pieces))
        return jnp.repeat(jnp.exp(steps), shape[axis_at] // parts).reshape((-1,) + (1,) * (len(shape) - axis_at - 1))

    gain = one(*pieces[0])
    for cut in pieces[1:]:
        gain = gain * one(*cut)
    return gain


def routed_block(stream_key, own, number, rows, number_of, top, bound, skew):
    sequence = jax.random.permutation(stream_key, number_of)
    heavy_load, usual = portions_of(number_of, rows * top, bound, skew, True), portions_of(number_of, rows * top, bound, skew, False)
    places = jnp.arange(number_of)

    def named(sizes, rotation):
        used = int((sizes > 0).sum())
        fixed = max(1, used // 4)
        moved = fixed + (places - fixed + rotation * (used - fixed)) % max(1, number_of - fixed)
        return jnp.zeros((number_of,), jnp.int32).at[sequence[jnp.where(places < fixed, places, moved)]].set(jnp.asarray(sizes, jnp.int32))

    sizes = jnp.where(number % 4 == 0, named(heavy_load, number // 4), named(usual, number - number // 4 - 1))
    mixed = jax.random.permutation(jax.random.fold_in(own, 3), number_of)
    source_of, receiver = mixed[0:number_of // 2 * 2:2], mixed[1:number_of // 2 * 2:2]
    margin = jnp.minimum(sizes[source_of] - 1, bound - sizes[receiver]) // 2
    margin = jnp.where((source_of == sequence[0]) | (receiver == sequence[0]) | (sizes[receiver] == 0), 0, jnp.maximum(margin, 0))
    moved = jax.random.randint(jax.random.fold_in(own, 4), (number_of // 2,), 0, 1 << 20) % (margin + 1)
    sizes = sizes.at[source_of].add(-moved).at[receiver].add(moved)
    items = jnp.searchsorted(jnp.cumsum(sizes), jnp.arange(rows * top), side="right").astype(jnp.int32)
    grid = items.reshape(top, rows).T
    grid = grid[jax.random.permutation(jax.random.fold_in(own, 1), rows)]
    rotation = jax.random.randint(jax.random.fold_in(own, 2), (rows, 1), 0, top)
    return jnp.take_along_axis(grid, (jnp.arange(top)[None, :] + rotation) % top, axis=1)


def portions_of(number_of, total, limit, slope, full):
    loads = [(1 << 20) // math.isqrt(rank ** slope) + 1 for rank in range(1, number_of + 1)]
    largest = limit if full else min(limit, max(-(-total // number_of), total * loads[0] // sum(loads)))
    least = 1 if total - largest >= number_of - 1 else 0
    counts, surplus = [largest] + [least] * (number_of - 1), total - largest - least * (number_of - 1)
    while surplus > 0:
        free = [i for i in range(1, number_of) if counts[i] < largest] or [i for i in range(1, number_of) if counts[i] < limit]
        pool, remaining = sum([loads[i] for i in free]), surplus
        for i in free:
            more = min(limit - counts[i], max(1, remaining * loads[i] // pool), surplus)
            counts[i] = counts[i] + more
            surplus = surplus - more
    return np.array(counts)


def centred(own_key, shape, scale, reach, split=(), kind=jnp.bfloat16):
    array = jax.random.normal(own_key, shape, jnp.float32) * scale
    if len(split) > 0:
        array = level_of(own_key, shape, split, -0.22, 0.18) * array
    return jnp.clip(array, min=-reach, max=reach).astype(kind)


def setup_inputs(seed: int = 0) -> dict:
    seeds = jax.random.split(jax.random.key(seed), 11)
    tokens = centred(seeds[0], (TOKENS, D), 1.0, 6.0, ((0, 32),))
    cotangent = centred(seeds[1], (TOKENS, D), 1.0, 6.0, ((0, 32),))
    routes_keys = jax.random.split(jax.random.fold_in(seeds[2], 1), TOKENS // TOK_DEV)
    routes_turns = jax.random.permutation(jax.random.fold_in(seeds[2], 3), TOKENS // TOK_DEV)
    routes = jax.vmap(lambda own, number: routed_block(jax.random.fold_in(seeds[2], 2), own, number, TOK_DEV, EXPERTS, TOP, CAP, 2))(routes_keys, routes_turns).reshape((TOKENS, TOP))
    combine_weights = jnp.clip(0.1 + 0.9 * jax.random.uniform(seeds[3], (TOKENS, TOP), jnp.float32) ** level_of(seeds[3], (TOKENS, TOP), ((0, 32),), -0.2, 0.2), 0.1, 1.0)
    gate_weight = centred(seeds[4], (EXPERTS, D, H), D ** -0.5, 0.09375, ((0, 8), (1, 4)))
    up_weight = centred(seeds[5], (EXPERTS, D, H), D ** -0.5, 0.09375, ((0, 8), (1, 4)))
    down_weight_t = centred(seeds[6], (EXPERTS, D, H), H ** -0.5, 0.1875, ((0, 8), (1, 4)))
    sketch_bucket = touch_ends(jax.random.randint(seeds[7], (D,), 0, SKETCH), jax.random.fold_in(seeds[7], 1), 0, SKETCH - 1).astype(jnp.int32)
    sketch_sign = touch_ends((jax.random.randint(seeds[8], (D,), 0, 2) < 1).astype(jnp.int32), jax.random.fold_in(seeds[8], 1), 0, 1)
    error_state = centred(seeds[9], (EXPERTS, N_DP, 3, SKETCH, H), 0.5, 4.0, ((0, 8), (1, 4)), jnp.float32)
    return {"tokens": tokens, "cotangent": cotangent, "routes": routes, "combine_weights": combine_weights, "gate_weight": gate_weight, "up_weight": up_weight, "down_weight_t": down_weight_t, "sketch_bucket": sketch_bucket, "sketch_sign": sketch_sign, "error_state": error_state}


def slot_table(block_routes, expert_count, capacity):
    flat_routes = block_routes.reshape(-1)
    entries = flat_routes.shape[0]
    hit_table = (flat_routes[:, None] == jnp.arange(expert_count, dtype=jnp.int32)[None, :]).astype(jnp.int32)
    positions = jnp.cumsum(hit_table, axis=0) - 1
    slot_index = jnp.sum(positions * hit_table, axis=1)
    targets = (flat_routes * capacity + slot_index).astype(jnp.int32)
    owners = jnp.full((expert_count * capacity,), entries, jnp.int32)
    owners = owners.at[targets].set(jnp.arange(entries, dtype=jnp.int32))
    return targets.reshape(block_routes.shape), owners


def contract_rows(left_side, right_side):
    return lax.dot_general(left_side, right_side, (((0,), (0,)), ((), ())), preferred_element_type=jnp.float32)


def contract_cols(left_side, right_side):
    return lax.dot_general(left_side, right_side, (((1,), (1,)), ((), ())), preferred_element_type=jnp.float32)


def expert_forward(rows_in, gate_w, up_w, down_w):
    gate_pre = jnp.dot(rows_in, gate_w, preferred_element_type=jnp.float32)
    up_pre = jnp.dot(rows_in, up_w, preferred_element_type=jnp.float32)
    hidden = (gate_pre * jax.nn.sigmoid(gate_pre) * up_pre).astype(jnp.bfloat16)
    rows_out = contract_cols(hidden, down_w).astype(jnp.bfloat16)
    return rows_out, hidden, gate_pre, up_pre


def expert_backward(rows_cot, gate_pre, up_pre, gate_w, up_w, down_w):
    hidden_cot = jnp.dot(rows_cot, down_w, preferred_element_type=jnp.float32)
    gate_sig = jax.nn.sigmoid(gate_pre)
    gate_cot = (hidden_cot * up_pre * gate_sig * (1.0 + gate_pre * (1.0 - gate_sig))).astype(jnp.bfloat16)
    up_cot = (hidden_cot * gate_pre * gate_sig).astype(jnp.bfloat16)
    rows_grad = (contract_cols(gate_cot, gate_w) + contract_cols(up_cot, up_w)).astype(jnp.bfloat16)
    return rows_grad, gate_cot, up_cot


def sketch_rows(matrix, sketch_bucket, sign_values):
    return jax.ops.segment_sum(matrix * sign_values[:, None], sketch_bucket, num_segments=SKETCH)


def feedback(sketched, error_now, tok_count):
    scaled = sketched * (4.0 / tok_count) + error_now
    threshold = jnp.mean(jnp.abs(scaled), axis=(1, 2), keepdims=True)
    kept_part = jnp.clip(scaled, -threshold, threshold)
    return scaled - kept_part, kept_part


def reference(tokens, cotangent, routes, combine_weights, gate_weight, up_weight, down_weight_t, sketch_bucket, sketch_sign, error_state):
    model_width = tokens.shape[1]
    top_count = routes.shape[1]
    entries = TOK_DEV * top_count
    sign_values = (2 * sketch_sign - 1).astype(jnp.float32)
    token_blocks = tokens.reshape(N_EXPERT, N_DP, TOK_DEV, model_width)
    cot_blocks = cotangent.reshape(N_EXPERT, N_DP, TOK_DEV, model_width)
    route_blocks = routes.reshape(N_EXPERT, N_DP, TOK_DEV, top_count)
    weight_blocks = combine_weights.reshape(N_EXPERT, N_DP, TOK_DEV, top_count)

    def take_rows(table_rows, index_rows):
        return table_rows[index_rows]

    def replica(replica_id):
        rep_tokens = token_blocks[:, replica_id]
        rep_cot = cot_blocks[:, replica_id]
        rep_routes = route_blocks[:, replica_id]
        rep_weights = weight_blocks[:, replica_id]
        targets, owners = jax.vmap(lambda block_rows: slot_table(block_rows, N_EXPERT, CAP))(rep_routes)
        live_rows = (owners < entries)[..., None]
        safe_index = jnp.minimum(owners, entries - 1)
        cot_entries = (rep_weights[..., None] * rep_cot[:, :, None, :].astype(jnp.float32)).astype(jnp.bfloat16)
        cot_entries = cot_entries.reshape(N_EXPERT, entries, model_width)
        zero_value = jnp.zeros((), jnp.bfloat16)
        token_send = jnp.where(live_rows, jax.vmap(take_rows)(rep_tokens, safe_index // top_count), zero_value)
        cot_send = jnp.where(live_rows, jax.vmap(take_rows)(cot_entries, safe_index), zero_value)
        token_send = token_send.reshape(N_EXPERT, N_EXPERT, CAP, model_width).transpose(1, 0, 2, 3)
        cot_send = cot_send.reshape(N_EXPERT, N_EXPERT, CAP, model_width).transpose(1, 0, 2, 3)

        def one_expert(carry_state, scanned):
            token_rows, cot_rows, gate_w, up_w, down_w, error_now = scanned
            rows_in = token_rows.reshape(-1, model_width)
            rows_cot = cot_rows.reshape(-1, model_width)
            rows_out, hidden, gate_pre, up_pre = expert_forward(rows_in, gate_w, up_w, down_w)
            rows_grad, gate_cot, up_cot = expert_backward(rows_cot, gate_pre, up_pre, gate_w, up_w, down_w)
            sketched = jnp.stack([
                sketch_rows(contract_rows(rows_in, gate_cot), sketch_bucket, sign_values),
                sketch_rows(contract_rows(rows_in, up_cot), sketch_bucket, sign_values),
                sketch_rows(contract_rows(rows_cot, hidden), sketch_bucket, sign_values)])
            sent_part, kept_part = feedback(sketched, error_now, TOK_DEV)
            return carry_state, (rows_out, rows_grad, sent_part, kept_part)

        scanned_in = (token_send, cot_send, gate_weight, up_weight, down_weight_t, error_state[:, replica_id])
        unused, results = lax.scan(one_expert, jnp.zeros((), jnp.float32), scanned_in)
        outs_all, grads_all, sent_all, kept_all = results
        outs_home = outs_all.reshape(N_EXPERT, N_EXPERT, CAP, model_width).transpose(1, 0, 2, 3)
        outs_home = outs_home.reshape(N_EXPERT, N_EXPERT * CAP, model_width)
        grads_home = grads_all.reshape(N_EXPERT, N_EXPERT, CAP, model_width).transpose(1, 0, 2, 3)
        grads_home = grads_home.reshape(N_EXPERT, N_EXPERT * CAP, model_width)
        picked = jax.vmap(take_rows)(outs_home, targets)
        picked_grad = jax.vmap(take_rows)(grads_home, targets)
        layer_out = jnp.sum(rep_weights[..., None] * picked.astype(jnp.float32), axis=2).astype(jnp.bfloat16)
        input_grad = jnp.sum(picked_grad.astype(jnp.float32), axis=2).astype(jnp.bfloat16)
        return layer_out, input_grad, sent_all, kept_all

    layer_out, input_grad, sent_all, kept_all = lax.map(replica, jnp.arange(N_DP, dtype=jnp.int32))
    layer_out = layer_out.transpose(1, 0, 2, 3).reshape(-1, model_width)
    input_grad = input_grad.transpose(1, 0, 2, 3).reshape(-1, model_width)
    sketch_total = jnp.sum(sent_all, axis=0)
    error_next = kept_all.transpose(1, 0, 2, 3, 4)
    return (layer_out, input_grad, sketch_total, error_next)
```

```python
import jax
import jax.numpy as jnp
from jax import lax
from jax.sharding import PartitionSpec as P

SKETCH = 128
F32 = jnp.float32
BF16 = jnp.bfloat16


def places_of(routes, expert_count, capacity):
    tok_count, top_count = routes.shape
    flat = routes.reshape(-1)
    entries = flat.shape[0]
    same = flat[:, None] == flat[None, :]
    index = jnp.arange(entries, dtype=jnp.int32)
    earlier = index[None, :] < index[:, None]
    slots = jnp.sum((same & earlier).astype(jnp.int32), axis=1)
    return (flat * capacity + slots).reshape(tok_count, top_count)


def contract_cols(left_side, right_side):
    return lax.dot_general(
        left_side, right_side, (((1,), (1,)), ((), ())), preferred_element_type=F32
    )


def contract_rows(left_side, right_side):
    return lax.dot_general(
        left_side, right_side, (((0,), (0,)), ((), ())), preferred_element_type=F32
    )


def exchange(rows, expert_count, capacity):
    width = rows.shape[1]
    return lax.all_to_all(
        rows.reshape(expert_count, capacity, width), "expert", 0, 0, tiled=True
    ).reshape(-1, width)


def feedback(sketched, error_now, tok_count):
    scaled = sketched * (4.0 / tok_count) + error_now
    threshold = jnp.mean(jnp.abs(scaled), axis=(1, 2), keepdims=True)
    kept_part = jnp.clip(scaled, -threshold, threshold)
    return (scaled - kept_part, kept_part)


def on_device(
    tokens,
    cotangent,
    routes,
    combine_weights,
    gate_weight,
    up_weight,
    down_weight_t,
    sketch_bucket,
    sketch_sign,
    error_state,
):
    expert_count = lax.axis_size("expert")
    tok_count = tokens.shape[0]
    entries = tok_count * routes.shape[1]
    capacity = entries * 9 // (8 * expert_count)
    gate_full = lax.all_gather(gate_weight, "dp", axis=1, tiled=True)[0]
    up_full = lax.all_gather(up_weight, "dp", axis=1, tiled=True)[0]
    down_full = lax.all_gather(down_weight_t, "dp", axis=1, tiled=True)[0]
    sign_values = (2 * sketch_sign - 1).astype(F32)
    bucket_hits = sketch_bucket[None, :] == jnp.arange(SKETCH, dtype=jnp.int32)[:, None]
    signed_table = jnp.where(bucket_hits, sign_values[None, :], 0.0).astype(BF16)
    places = places_of(routes, expert_count, capacity)
    place_ids = jnp.arange(expert_count * capacity, dtype=jnp.int32)
    hits = [places[:, k][None, :] == place_ids[:, None] for k in range(2)]
    both = (hits[0] | hits[1]).astype(BF16)
    one_hot = [h.astype(BF16) for h in hits]
    row_weight = sum(
        jnp.sum(jnp.where(hits[k], combine_weights[:, k][None, :], 0.0), axis=1) for k in range(2)
    )
    token_send = jnp.dot(both, tokens, preferred_element_type=F32).astype(BF16)
    rows_in = exchange(token_send, expert_count, capacity)
    cot_send = (
        row_weight[:, None] * jnp.dot(both, cotangent, preferred_element_type=F32)
    ).astype(BF16)
    rows_cot = exchange(cot_send, expert_count, capacity)
    gate_pre = jnp.dot(rows_in, gate_full, preferred_element_type=F32)
    up_pre = jnp.dot(rows_in, up_full, preferred_element_type=F32)
    gate_sig = jax.nn.sigmoid(gate_pre)
    hidden = (gate_pre * gate_sig * up_pre).astype(BF16)
    rows_out = contract_cols(hidden, down_full).astype(BF16)
    returned = exchange(rows_out, expert_count, capacity)
    hidden_cot = jnp.dot(rows_cot, down_full, preferred_element_type=F32)
    gate_cot = (hidden_cot * up_pre * gate_sig * (1.0 + gate_pre * (1.0 - gate_sig))).astype(BF16)
    up_cot = (hidden_cot * gate_pre * gate_sig).astype(BF16)
    rows_grad = (contract_cols(gate_cot, gate_full) + contract_cols(up_cot, up_full)).astype(BF16)
    grad_home = exchange(rows_grad, expert_count, capacity)
    folded_in = contract_cols(signed_table, rows_in)
    folded_cot = contract_cols(signed_table, rows_cot)
    highest = lax.Precision.HIGHEST
    sketched = jnp.stack(
        [
            jnp.dot(folded_in, gate_cot.astype(F32), precision=highest),
            jnp.dot(folded_in, up_cot.astype(F32), precision=highest),
            jnp.dot(folded_cot, hidden.astype(F32), precision=highest),
        ]
    )
    sent_part, kept_part = feedback(sketched, error_state[0, 0], tok_count)
    sketch_total = lax.psum(sent_part, "dp")
    picked = [contract_rows(one_hot[k], returned) for k in range(2)]
    layer_out = (
        combine_weights[:, 0:1] * picked[0] + combine_weights[:, 1:2] * picked[1]
    ).astype(BF16)
    input_grad = contract_rows(both, grad_home).astype(BF16)
    return (layer_out, input_grad, sketch_total[None], kept_part[None, None])


def solution(mesh):
    in_specs = (
        P(("expert", "dp"), None),
        P(("expert", "dp"), None),
        P(("expert", "dp"), None),
        P(("expert", "dp"), None),
        P("expert", "dp", None),
        P("expert", "dp", None),
        P("expert", "dp", None),
        P(),
        P(),
        P("expert", "dp", None, None, None),
    )
    out_specs = (
        P(("expert", "dp"), None),
        P(("expert", "dp"), None),
        P("expert", None, None, None),
        P("expert", "dp", None, None, None),
    )
    return jax.shard_map(
        on_device, mesh=mesh, in_specs=in_specs, out_specs=out_specs, check_vma=False
    )
```

```python
import functools

import jax
import jax.numpy as jnp
from jax import lax
from jax.experimental import pallas as pl
from jax.experimental.pallas import tpu as pltpu
from jax.sharding import PartitionSpec as P

SKETCH = 128
TILE = 256
CHUNKS = 2
F32 = jnp.float32
BF16 = jnp.bfloat16
MESH = pl.DeviceIdType.MESH


def mul(a, b):
    return lax.dot_general(a, b, (((1,), (0,)), ((), ())), preferred_element_type=F32)


def mul_t(a, b):
    return lax.dot_general(a, b, (((1,), (1,)), ((), ())), preferred_element_type=F32)


def t_mul(a, b):
    return lax.dot_general(a, b, (((0,), (0,)), ((), ())), preferred_element_type=F32)


def aligned(value, by):
    return pl.multiple_of(value, by)


class Plan:
    def __init__(self, experts, replicas, tokens, width, hidden):
        self.experts, self.replicas = experts, replicas
        self.tokens, self.width, self.hidden = tokens, width, hidden
        self.chips = replicas // 2
        self.shard = width // replicas
        self.cap = tokens * 2 * 9 // (8 * experts)
        self.main = self.cap // 16 * 16
        self.rest = self.cap - self.main
        self.pieces = 16 // self.rest
        self.piece = width // self.pieces
        self.main_rows = experts * self.main
        self.rest_rows = experts * self.rest
        self.rows = self.main_rows + self.rest_rows
        self.ext_rows = experts * 16
        fine = (width // self.chips) % TILE == 0
        self.groups = self.chips if fine else 1
        self.columns = width // self.groups
        away = experts - 1
        self.copies = (
            4 * away
            + (self.groups + 1) * away
            + 3 * away
            + 3 * CHUNKS * (2 * self.chips - 1)
            + self.chips
            + 1
        )


def kernel(
    p,
    tokens,
    cotangent,
    routes,
    routes_t,
    weights,
    weights_t,
    gate_shard,
    up_shard,
    down_shard,
    bucket,
    sign,
    error,
    layer_out,
    input_grad,
    total_out,
    kept_out,
    gate_w,
    up_w,
    down_w,
    x_in,
    c_in,
    a_send,
    b_send,
    a_ext,
    b_ext,
    x_ext,
    c_ext,
    y_home,
    g_home,
    y_ext,
    g_ext,
    gate_pre,
    up_pre,
    hidden_cot,
    hidden,
    gate_cot,
    up_cot,
    table,
    fold_x,
    fold_c,
    sent,
    pair,
    chip_sums,
    total_half,
    send_sems,
    recv_sems,
    local_sems,
):
    me = lax.axis_index("expert")
    replica = lax.axis_index("dp")
    chip, core = replica // 2, replica % 2
    sibling = {"dp": chip * 2 + 1 - core}
    experts, chips, cap, main, rest = p.experts, p.chips, p.cap, p.main, p.rest
    used = [0]

    def remote(source, target, device):
        at = used[0]
        used[0] += 1
        copy = pltpu.make_async_remote_copy(
            src_ref=source,
            dst_ref=target,
            send_sem=send_sems.at[at],
            recv_sem=recv_sems.at[at],
            device_id=device,
            device_id_type=MESH,
        )
        copy.start()
        return copy

    def peer(k):
        return lax.rem(me + k, experts)

    def twin(k):
        return {"dp": lax.rem(chip + k, chips) * 2 + core}

    barrier = pltpu.get_barrier_semaphore()
    for k in range(1, experts):
        pl.semaphore_signal(
            barrier, inc=1, device_id={"expert": peer(k)}, device_id_type=MESH
        )
    pl.semaphore_signal(barrier, inc=1, device_id=sibling, device_id_type=MESH)
    for k in range(1, chips):
        pl.semaphore_signal(barrier, inc=1, device_id=twin(k), device_id_type=MESH)
    pl.semaphore_wait(barrier, experts + chips - 1)

    outgoing = []

    def rows_of(full, owner, chunk):
        size = p.shard // CHUNKS
        return full.at[pl.ds(aligned(owner * p.shard + chunk * size, 16), size)]

    def send_shard(shard, full):
        size = p.shard // CHUNKS
        far, near = [], []
        for chunk in range(CHUNKS):
            source = shard.at[0, pl.ds(chunk * size, size)]
            target = rows_of(full, replica, chunk)
            far.append([remote(source, target, twin(k)) for k in range(1, chips)])
            near.append(remote(source, target, sibling))
        outgoing.extend(near + [c for f in far for c in f])
        return far, near

    def forward(full, far):
        forwarded = []
        for chunk in range(CHUNKS):
            for k in range(1, chips):
                far[chunk][k - 1].wait_recv()
                owner = lax.rem(chip + chips - k, chips) * 2 + core
                block = rows_of(full, owner, chunk)
                forwarded.append(remote(block, block, sibling))
        outgoing.extend(forwarded)
        return forwarded

    own = []
    for i, (shard, full) in enumerate(
        ((gate_shard, gate_w), (up_shard, up_w), (down_shard, down_w))
    ):
        copy = pltpu.make_async_copy(
            shard.at[0],
            full.at[pl.ds(aligned(replica * p.shard, 16), p.shard)],
            local_sems.at[i],
        )
        copy.start()
        own.append(copy)
    error_copy = pltpu.make_async_copy(error.at[0, 0], sent, local_sems.at[3])
    error_copy.start()
    gate_far, gate_near = send_shard(gate_shard, gate_w)
    up_far, up_near = send_shard(up_shard, up_w)

    count = p.tokens
    first = lax.broadcasted_iota(jnp.int32, (count, count), 0)
    second = lax.broadcasted_iota(jnp.int32, (count, count), 1)
    across, down_rows = [], []
    for k in range(2):
        lane_expert = routes_t[k : k + 1, :]
        row_expert = routes[:, k : k + 1]
        lane_slot = jnp.zeros((1, count), jnp.int32)
        row_slot = jnp.zeros((count, 1), jnp.int32)
        for j in range(2):
            same = (routes[:, j : j + 1] == lane_expert) & (first < second)
            lane_slot += jnp.sum(same.astype(jnp.int32), axis=0, keepdims=True)
            same = (routes_t[j : j + 1, :] == row_expert) & (second < first)
            row_slot += jnp.sum(same.astype(jnp.int32), axis=1, keepdims=True)
        across.append((lane_expert, lane_slot))
        down_rows.append((row_expert, row_slot))

    def main_index(expert, slot):
        return jnp.where(slot < main, expert * main + slot, -1)

    def ext_index(expert, slot, piece):
        return jnp.where(slot < main, -1, expert * 16 + piece * rest + slot - main)

    main_ids = lax.broadcasted_iota(jnp.int32, (p.main_rows, count), 0)
    ext_ids = lax.broadcasted_iota(jnp.int32, (p.ext_rows, count), 0)
    main_hits = [main_ids == main_index(*across[k]) for k in range(2)]
    ext_hits = [
        [ext_ids == ext_index(*across[k], piece) for k in range(2)] for piece in range(p.pieces)
    ]

    def as_bf16(hit):
        return jnp.where(hit, 1.0, 0.0).astype(BF16)

    pick_main = as_bf16(main_hits[0] | main_hits[1])
    pick_ext = [as_bf16(h[0] | h[1]) for h in ext_hits]

    def weigh(hits):
        return sum(
            jnp.sum(jnp.where(hits[k], weights_t[k : k + 1, :], 0.0), axis=1, keepdims=True)
            for k in range(2)
        )

    main_weight = weigh(main_hits)
    ext_weight = sum(weigh(h) for h in ext_hits)

    def piece_of(i):
        return slice(i * p.piece, (i + 1) * p.piece)

    def block_rows(i, size):
        return pl.ds(aligned(i * size, 16), size)

    def spread(source, target, size, columns=None):
        copies = []
        for k in range(1, experts):
            there, here = block_rows(peer(k), size), block_rows(me, size)
            if columns is None:
                src, dst = source.at[there], target.at[here]
            else:
                src, dst = source.at[there, columns], target.at[here, columns]
            copies.append(remote(src, dst, {"expert": peer(k)}))
        outgoing.extend(copies)
        return copies

    def keep(source, target, size):
        here = block_rows(me, size)
        target[here, :] = source[here, :]

    def arrive(copies):
        for copy in copies:
            copy.wait_recv()

    def dispatch(rows, send, ext, landing, landing_ext, main_scale, ext_scale):
        for i in range(p.pieces):
            block = mul(pick_main, rows[:, piece_of(i)])
            if main_scale is not None:
                block = block * main_scale
            send[0 : p.main_rows, piece_of(i)] = block.astype(BF16)
        copies = spread(send, landing, main)
        packed = sum(mul(pick_ext[i], rows[:, piece_of(i)]) for i in range(p.pieces))
        if ext_scale is not None:
            packed = packed * ext_scale
        ext[...] = packed.astype(BF16)
        copies += spread(ext, landing_ext, 16)
        keep(send, landing, main)
        keep(ext, landing_ext, 16)
        return copies

    x_copies = dispatch(tokens, a_send, a_ext, x_in, x_ext, None, None)
    c_copies = dispatch(cotangent, b_send, b_ext, c_in, c_ext, main_weight, ext_weight)

    bucket_ids = lax.broadcasted_iota(jnp.int32, (SKETCH, p.piece), 0)
    for i in range(p.pieces):
        signs = (2 * sign[:, piece_of(i)] - 1).astype(F32)
        table[:, piece_of(i)] = jnp.where(
            bucket[:, piece_of(i)] == bucket_ids, signs, 0.0
        ).astype(BF16)

    rest_ids = lax.broadcasted_iota(jnp.int32, (p.rest_rows, p.ext_rows), 0)
    packed_ids = lax.broadcasted_iota(jnp.int32, (p.rest_rows, p.ext_rows), 1)
    packed_at = rest_ids // rest * 16 + rest_ids % rest
    moves = [as_bf16(packed_ids == packed_at + i * rest) for i in range(p.pieces)]

    def unpack(ext, full):
        for i in range(p.pieces):
            full[p.main_rows : p.rows, piece_of(i)] = mul(moves[i], ext[...]).astype(BF16)

    def pack(full, ext):
        ext[...] = sum(
            t_mul(moves[i], full[p.main_rows : p.rows, piece_of(i)]) for i in range(p.pieces)
        ).astype(BF16)

    gate_forwarded = forward(gate_w, gate_far)
    down_far, down_near = send_shard(down_shard, down_w)
    up_forwarded = forward(up_w, up_far)
    arrive(x_copies)
    unpack(x_ext, x_in)
    fold_x[...] = mul_t(table[...], x_in[...])
    own[0].wait()
    own[1].wait()
    arrive(gate_near + up_near)
    arrive(gate_forwarded + up_forwarded)

    @pl.loop(0, p.hidden // TILE)
    def _(t):
        at = pl.ds(aligned(t * TILE, TILE), TILE)
        gate = mul(x_in[...], gate_w[:, at])
        up = mul(x_in[...], up_w[:, at])
        gate_pre[:, at] = gate
        up_pre[:, at] = up
        hidden[:, at] = (gate * jax.nn.sigmoid(gate) * up).astype(BF16)

    for copy in x_copies:
        copy.wait_send()
    own[2].wait()
    arrive(down_near)

    def group_start(g):
        if p.groups == 1:
            return 0
        return lax.rem(chip + g, chips) * p.columns

    def project(g):
        start = group_start(g)

        @pl.loop(0, p.columns // TILE)
        def _(t):
            at = pl.ds(aligned(start + t * TILE, TILE), TILE)
            a_send[:, at] = mul_t(hidden[...], down_w[at, :]).astype(BF16)

        return spread(a_send, y_home, main, pl.ds(aligned(start, TILE), p.columns))

    def back(g):
        at_rows = pl.ds(aligned(group_start(g), TILE), p.columns)

        @pl.loop(0, p.hidden // TILE)
        def _(t):
            at = pl.ds(aligned(t * TILE, TILE), TILE)
            part = mul(c_in[:, at_rows], down_w[at_rows, at])
            if g == 0:
                hidden_cot[:, at] = part
            else:
                hidden_cot[:, at] += part

    def cot_arrives():
        arrive(c_copies)
        unpack(c_ext, c_in)
        fold_c[...] = mul_t(table[...], c_in[...])

    if p.groups > 1:
        y_copies = project(0)
        cot_arrives()
        back(0)
        down_forwarded = forward(down_w, down_far)
        arrive(down_forwarded)
        for g in range(1, p.groups):
            y_copies += project(g)
    else:
        cot_arrives()
        down_forwarded = forward(down_w, down_far)
        arrive(down_forwarded)
        y_copies = project(0)
        back(0)
    pack(a_send, a_ext)
    y_copies += spread(a_ext, y_ext, 16)
    for g in range(1, p.groups):
        back(g)

    @pl.loop(0, p.hidden // TILE)
    def _(t):
        at = pl.ds(aligned(t * TILE, TILE), TILE)
        gate, cot = gate_pre[:, at], hidden_cot[:, at]
        sig = jax.nn.sigmoid(gate)
        gate_cot[:, at] = (cot * up_pre[:, at] * sig * (1.0 + gate * (1.0 - sig))).astype(BF16)
        up_cot[:, at] = (cot * gate * sig).astype(BF16)

    for copy in c_copies:
        copy.wait_send()
    half = p.width // 2
    g_halves = []
    for h in range(2):

        @pl.loop(0, half // TILE)
        def _(t):
            at = pl.ds(aligned(h * half + t * TILE, TILE), TILE)
            b_send[:, at] = (
                mul_t(gate_cot[...], gate_w[at, :]) + mul_t(up_cot[...], up_w[at, :])
            ).astype(BF16)

        g_halves.append(spread(b_send, g_home, main, pl.ds(h * half, half)))
    pack(b_send, b_ext)
    g_rest = spread(b_ext, g_ext, 16)
    keep(a_send, y_home, main)
    keep(a_ext, y_ext, 16)
    keep(b_send, g_home, main)
    keep(b_ext, g_ext, 16)

    error_copy.wait()
    for m, (fold, right) in enumerate(((fold_x, gate_cot), (fold_x, up_cot), (fold_c, hidden))):
        high = fold[...].astype(BF16)
        low = (fold[...] - high.astype(F32)).astype(BF16)
        sketched = mul(high, right[...]) + mul(low, right[...])
        scaled = sketched * (4.0 / p.tokens) + sent[m]
        threshold = jnp.sum(jnp.abs(scaled)) / (SKETCH * p.hidden)
        kept = jnp.clip(scaled, -threshold, threshold)
        kept_out[0, 0, m] = kept
        sent[m] = scaled - kept
    mid = p.hidden // 2
    mine = pl.ds(aligned(core * mid, mid), mid)
    theirs = pl.ds(aligned((1 - core) * mid, mid), mid)
    pair_copy = remote(sent.at[:, :, theirs], pair, sibling)
    pair_copy.wait_recv()
    chip_sums[chip] = sent[:, :, mine] + pair[...]
    chip_copies = [
        remote(chip_sums.at[chip], chip_sums.at[chip], twin(k)) for k in range(1, chips)
    ]

    arrive(y_copies)
    lane_main = lax.broadcasted_iota(jnp.int32, (count, p.main_rows), 1)
    lane_ext = lax.broadcasted_iota(jnp.int32, (count, p.ext_rows), 1)
    home_main = [lane_main == main_index(*down_rows[k]) for k in range(2)]
    for i in range(p.pieces):
        value = 0.0
        for k in range(2):
            hit = lane_ext == ext_index(*down_rows[k], i)
            picked = mul(as_bf16(home_main[k]), y_home[:, piece_of(i)])
            picked += mul(as_bf16(hit), y_ext[...])
            value += weights[:, k : k + 1] * picked
        layer_out[:, piece_of(i)] = value.astype(BF16)

    for copy in chip_copies:
        copy.wait_recv()
    pair_copy.wait_send()
    sent[:, :, mine] = functools.reduce(lambda a, b: a + b, [chip_sums[i] for i in range(chips)])
    total_copy = remote(sent.at[:, :, mine], total_half, sibling)
    results = [
        pltpu.make_async_copy(sent.at[:, :, mine], total_out.at[0, :, :, mine], local_sems.at[0])
    ]
    results[0].start()

    both_main = as_bf16(home_main[0] | home_main[1])
    arrive(g_rest)
    arrive(g_halves[0])
    for i in range(p.pieces):
        if i * 2 == p.pieces:
            arrive(g_halves[1])
        hit = (lane_ext == ext_index(*down_rows[0], i)) | (
            lane_ext == ext_index(*down_rows[1], i)
        )
        value = mul(both_main, g_home[:, piece_of(i)]) + mul(as_bf16(hit), g_ext[...])
        input_grad[:, piece_of(i)] = value.astype(BF16)

    total_copy.wait_recv()
    total_copy.wait_send()
    results.append(
        pltpu.make_async_copy(total_half, total_out.at[0, :, :, theirs], local_sems.at[1])
    )
    results[1].start()
    waited = {id(c) for c in x_copies + c_copies}
    for copy in outgoing + chip_copies:
        if id(copy) not in waited:
            copy.wait_send()
    for result in results:
        result.wait()


def on_device(
    experts,
    replicas,
    tokens,
    cotangent,
    routes,
    combine_weights,
    gate_weight,
    up_weight,
    down_weight_t,
    sketch_bucket,
    sketch_sign,
    error_state,
):
    count, width = tokens.shape
    units = gate_weight.shape[2]
    p = Plan(experts, replicas, count, width, units)
    vmem = pl.BlockSpec(memory_space=pltpu.VMEM)
    hbm = pl.BlockSpec(memory_space=pl.ANY)
    stage = (3, SKETCH, units)
    return pl.pallas_call(
        functools.partial(kernel, p),
        out_shape=(
            jax.ShapeDtypeStruct((count, width), BF16),
            jax.ShapeDtypeStruct((count, width), BF16),
            jax.ShapeDtypeStruct((1,) + stage, F32),
            jax.ShapeDtypeStruct((1, 1) + stage, F32),
        ),
        in_specs=[vmem] * 6 + [hbm] * 3 + [vmem] * 2 + [hbm],
        out_specs=(vmem, vmem, hbm, vmem),
        scratch_shapes=[pltpu.VMEM((width, units), BF16)] * 3
        + [pltpu.VMEM((p.rows, width), BF16)] * 4
        + [pltpu.VMEM((p.ext_rows, p.piece), BF16)] * 4
        + [pltpu.VMEM((p.main_rows, width), BF16)] * 2
        + [pltpu.VMEM((p.ext_rows, p.piece), BF16)] * 2
        + [pltpu.VMEM((p.rows, units), F32)] * 3
        + [pltpu.VMEM((p.rows, units), BF16)] * 3
        + [pltpu.VMEM((SKETCH, width), BF16)]
        + [pltpu.VMEM((SKETCH, p.rows), F32)] * 2
        + [
            pltpu.VMEM(stage, F32),
            pltpu.VMEM((3, SKETCH, units // 2), F32),
            pltpu.VMEM((p.chips, 3, SKETCH, units // 2), F32),
            pltpu.VMEM((3, SKETCH, units // 2), F32),
            pltpu.SemaphoreType.DMA((p.copies,)),
            pltpu.SemaphoreType.DMA((p.copies,)),
            pltpu.SemaphoreType.DMA((4,)),
        ],
        compiler_params=pltpu.CompilerParams(
            collective_id=0, has_side_effects=True, vmem_limit_bytes=63 * 2**20
        ),
    )(
        tokens,
        cotangent,
        routes,
        routes.T,
        combine_weights,
        combine_weights.T,
        gate_weight,
        up_weight,
        down_weight_t,
        sketch_bucket[None],
        sketch_sign[None],
        error_state,
    )


def solution(mesh):
    in_specs = (
        P(("expert", "dp"), None),
        P(("expert", "dp"), None),
        P(("expert", "dp"), None),
        P(("expert", "dp"), None),
        P("expert", "dp", None),
        P("expert", "dp", None),
        P("expert", "dp", None),
        P(),
        P(),
        P("expert", "dp", None, None, None),
    )
    out_specs = (
        P(("expert", "dp"), None),
        P(("expert", "dp"), None),
        P("expert", None, None, None),
        P("expert", "dp", None, None, None),
    )
    body = functools.partial(on_device, mesh.shape["expert"], mesh.shape["dp"])
    return jax.shard_map(body, mesh=mesh, in_specs=in_specs, out_specs=out_specs, check_vma=False)
```

```python
import functools

import jax
import jax.numpy as jnp
from jax import lax
from jax.experimental import pallas as pl
from jax.experimental.pallas import tpu as pltpu
from jax.sharding import PartitionSpec as P

SKETCH = 128
TILE = 256
CHUNKS = 2
LANES = 128
F32 = jnp.float32
BF16 = jnp.bfloat16
MESH = pl.DeviceIdType.MESH


def mul(a, b):
    return lax.dot_general(a, b, (((1,), (0,)), ((), ())), preferred_element_type=F32)


def mul_t(a, b):
    return lax.dot_general(a, b, (((1,), (1,)), ((), ())), preferred_element_type=F32)


def t_mul(a, b):
    return lax.dot_general(a, b, (((0,), (0,)), ((), ())), preferred_element_type=F32)


def aligned(value, by):
    return pl.multiple_of(value, by)


class Plan:
    def __init__(self, experts, replicas, tokens, width, hidden):
        self.experts, self.replicas = experts, replicas
        self.tokens, self.width, self.hidden = tokens, width, hidden
        self.chips = replicas // 2
        self.shard = width // replicas
        self.cap = tokens * 2 * 9 // (8 * experts)
        self.main = self.cap // 16 * 16
        self.rest = self.cap - self.main
        self.pieces = 16 // self.rest
        self.piece = width // self.pieces
        self.step = 1 if self.piece % LANES == 0 else self.pieces // 2
        self.main_rows = experts * self.main
        self.rest_rows = experts * self.rest
        self.rows = self.main_rows + self.rest_rows
        self.ext_rows = experts * 16
        fine = (width // self.chips) % TILE == 0
        self.groups = self.chips if fine else 1
        self.columns = width // self.groups
        half = self.shard // 2
        first = -(-half // TILE) * TILE if fine else half
        self.chunks = ((0, first), (first, self.shard - first))
        away = experts - 1
        self.copies = (
            (3 + self.pieces) * away
            + (2 * CHUNKS * (self.chips - 1) + 2) * away
            + 3 * away
            + 3 * CHUNKS * (2 * self.chips - 1)
            + self.chips
            + 1
        )


def kernel(
    p,
    tokens,
    cotangent,
    routes_t,
    weights_t,
    gate_shard,
    up_shard,
    down_shard,
    bucket,
    sign,
    error,
    layer_out,
    input_grad,
    total_out,
    kept_out,
    gate_w,
    up_w,
    down_w,
    x_in,
    c_in,
    a_send,
    b_send,
    a_ext,
    b_ext,
    x_ext,
    c_ext,
    y_home,
    g_home,
    y_ext,
    g_ext,
    gate_pre,
    up_pre,
    hidden_cot,
    hidden,
    gate_cot,
    up_cot,
    table,
    fold_x,
    fold_c,
    sent,
    pair,
    chip_sums,
    total_half,
    send_sems,
    recv_sems,
    local_sems,
):
    me = lax.axis_index("expert")
    replica = lax.axis_index("dp")
    chip, core = replica // 2, replica % 2
    sibling = {"dp": chip * 2 + 1 - core}
    experts, chips, cap, main, rest = p.experts, p.chips, p.cap, p.main, p.rest
    used = [0]

    def remote(source, target, device):
        at = used[0]
        used[0] += 1
        copy = pltpu.make_async_remote_copy(
            src_ref=source,
            dst_ref=target,
            send_sem=send_sems.at[at],
            recv_sem=recv_sems.at[at],
            device_id=device,
            device_id_type=MESH,
        )
        copy.start()
        return copy

    def peer(k):
        return lax.rem(me + k, experts)

    def twin(k):
        return {"dp": lax.rem(chip + k, chips) * 2 + core}

    barrier = pltpu.get_barrier_semaphore()
    for k in range(1, experts):
        pl.semaphore_signal(
            barrier, inc=1, device_id={"expert": peer(k)}, device_id_type=MESH
        )
    pl.semaphore_signal(barrier, inc=1, device_id=sibling, device_id_type=MESH)
    for k in range(1, chips):
        pl.semaphore_signal(barrier, inc=1, device_id=twin(k), device_id_type=MESH)
    pl.semaphore_wait(barrier, experts + chips - 1)

    outgoing = []

    def rows_of(full, owner, chunk):
        start, size = p.chunks[chunk]
        return full.at[pl.ds(aligned(owner * p.shard + start, 16), size)]

    def send_near(shard, full):
        copy = remote(
            shard.at[0], full.at[pl.ds(aligned(replica * p.shard, 16), p.shard)], sibling
        )
        outgoing.append(copy)
        return [copy]

    def send_far(shard, full, chunk):
        start, size = p.chunks[chunk]
        source = shard.at[0, pl.ds(start, size)]
        target = rows_of(full, replica, chunk)
        copies = [remote(source, target, twin(k)) for k in range(1, chips)]
        outgoing.extend(copies)
        return copies

    def forward(full, chunk, far):
        forwarded = []
        for k in range(1, chips):
            far[k - 1].wait_recv()
            owner = lax.rem(chip + chips - k, chips) * 2 + core
            block = rows_of(full, owner, chunk)
            forwarded.append(remote(block, block, sibling))
        outgoing.extend(forwarded)
        return forwarded

    own = []
    for i, (shard, full) in enumerate(
        ((gate_shard, gate_w), (up_shard, up_w), (down_shard, down_w))
    ):
        copy = pltpu.make_async_copy(
            shard.at[0],
            full.at[pl.ds(aligned(replica * p.shard, 16), p.shard)],
            local_sems.at[i],
        )
        copy.start()
        own.append(copy)
    error_copy = pltpu.make_async_copy(error.at[0, 0], sent, local_sems.at[3])
    error_copy.start()
    gate_far = [send_far(gate_shard, gate_w, chunk) for chunk in range(CHUNKS)]
    up_far = [send_far(up_shard, up_w, 0)]

    count = p.tokens
    first = lax.broadcasted_iota(jnp.int32, (count, count), 0)
    second = lax.broadcasted_iota(jnp.int32, (count, count), 1)
    across, down_rows, weights = [], [], []
    diagonal = first == second

    def stand(row):
        return jnp.sum(jnp.where(diagonal, row, jnp.zeros_like(row)), axis=1, keepdims=True)

    lane_experts = [routes_t[k : k + 1, :] for k in range(2)]
    row_experts = [stand(row) for row in lane_experts]
    for k in range(2):
        lane_expert, row_expert = lane_experts[k], row_experts[k]
        weights.append(stand(weights_t[k : k + 1, :]))
        lane_slot = jnp.zeros((1, count), jnp.int32)
        row_slot = jnp.zeros((count, 1), jnp.int32)
        for j in range(2):
            same = (row_experts[j] == lane_expert) & (first < second)
            lane_slot += jnp.sum(same.astype(jnp.int32), axis=0, keepdims=True)
            same = (lane_experts[j] == row_expert) & (second < first)
            row_slot += jnp.sum(same.astype(jnp.int32), axis=1, keepdims=True)
        across.append((lane_expert, lane_slot))
        down_rows.append((row_expert, row_slot))

    def main_index(expert, slot):
        return jnp.where(slot < main, expert * main + slot, -1)

    def ext_index(expert, slot, piece):
        return jnp.where(slot < main, -1, expert * 16 + piece * rest + slot - main)

    main_ids = lax.broadcasted_iota(jnp.int32, (p.main_rows, count), 0)
    ext_ids = lax.broadcasted_iota(jnp.int32, (p.ext_rows, count), 0)
    main_hits = [main_ids == main_index(*across[k]) for k in range(2)]
    ext_hits = [
        [ext_ids == ext_index(*across[k], piece) for k in range(2)] for piece in range(p.pieces)
    ]

    def as_bf16(hit):
        return jnp.where(hit, 1.0, 0.0).astype(BF16)

    pick_main = as_bf16(main_hits[0] | main_hits[1])
    pick_ext = [as_bf16(h[0] | h[1]) for h in ext_hits]

    def weigh(hits):
        return sum(
            jnp.sum(jnp.where(hits[k], weights_t[k : k + 1, :], 0.0), axis=1, keepdims=True)
            for k in range(2)
        )

    def piece_of(i):
        return slice(i * p.piece, (i + 1) * p.piece)

    def block_rows(i, size):
        return pl.ds(aligned(i * size, 16), size)

    def spread(source, target, size, columns=None):
        copies = []
        for k in range(1, experts):
            there, here = block_rows(peer(k), size), block_rows(me, size)
            if columns is None:
                src, dst = source.at[there], target.at[here]
            else:
                src, dst = source.at[there, columns], target.at[here, columns]
            copies.append(remote(src, dst, {"expert": peer(k)}))
        outgoing.extend(copies)
        return copies

    def keep(source, target, size):
        here = block_rows(me, size)
        target[here, :] = source[here, :]

    def arrive(copies):
        for copy in copies:
            copy.wait_recv()

    def dispatch(rows, send, ext, landing, landing_ext, main_scale, ext_scale):
        copies = []
        for i in range(p.pieces):
            block = mul(pick_main, rows[:, piece_of(i)])
            if main_scale is not None:
                block = block * main_scale
            send[0 : p.main_rows, piece_of(i)] = block.astype(BF16)
            cut = p.piece * p.step
            if main_scale is None and (i + 1) % p.step == 0:
                copies += spread(send, landing, main, pl.ds((i + 1) * p.piece - cut, cut))
        if main_scale is not None:
            copies = spread(send, landing, main)
        packed = sum(mul(pick_ext[i], rows[:, piece_of(i)]) for i in range(p.pieces))
        if ext_scale is not None:
            packed = packed * ext_scale
        ext[...] = packed.astype(BF16)
        copies += spread(ext, landing_ext, 16)
        keep(send, landing, main)
        keep(ext, landing_ext, 16)
        return copies

    x_copies = dispatch(tokens, a_send, a_ext, x_in, x_ext, None, None)
    main_weight = weigh(main_hits)
    ext_weight = sum(weigh(h) for h in ext_hits)
    c_copies = dispatch(cotangent, b_send, b_ext, c_in, c_ext, main_weight, ext_weight)

    bucket_ids = lax.broadcasted_iota(jnp.int32, (SKETCH, LANES), 0)
    for i in range(p.width // LANES):
        signs = (2 * sign[i : i + 1, :] - 1).astype(F32)
        table[:, i * LANES : (i + 1) * LANES] = jnp.where(
            bucket[i : i + 1, :] == bucket_ids, signs, 0.0
        ).astype(BF16)

    rest_ids = lax.broadcasted_iota(jnp.int32, (p.rest_rows, p.ext_rows), 0)
    packed_ids = lax.broadcasted_iota(jnp.int32, (p.rest_rows, p.ext_rows), 1)
    packed_at = rest_ids // rest * 16 + rest_ids % rest
    moves = [as_bf16(packed_ids == packed_at + i * rest) for i in range(p.pieces)]

    def unpack(ext, full):
        for i in range(p.pieces):
            full[p.main_rows : p.rows, piece_of(i)] = mul(moves[i], ext[...]).astype(BF16)

    def pack(full, ext):
        ext[...] = sum(
            t_mul(moves[i], full[p.main_rows : p.rows, piece_of(i)]) for i in range(p.pieces)
        ).astype(BF16)

    near = send_near(gate_shard, gate_w) + send_near(up_shard, up_w)
    down_near = send_near(down_shard, down_w)
    forwarded = forward(gate_w, 0, gate_far[0])
    up_far.append(send_far(up_shard, up_w, 1))
    forwarded += forward(gate_w, 1, gate_far[1])
    down_far = [send_far(down_shard, down_w, 0)]
    forwarded += forward(up_w, 0, up_far[0])
    forwarded += forward(up_w, 1, up_far[1])
    down_far.append(send_far(down_shard, down_w, 1))
    arrive(x_copies)
    unpack(x_ext, x_in)
    fold_x[...] = mul_t(table[...], x_in[...])
    own[0].wait()
    own[1].wait()
    arrive(near)
    arrive(forwarded)

    @pl.loop(0, p.hidden // TILE)
    def _(t):
        at = pl.ds(aligned(t * TILE, TILE), TILE)
        gate = mul(x_in[...], gate_w[:, at])
        up = mul(x_in[...], up_w[:, at])
        gate_pre[:, at] = gate
        up_pre[:, at] = up
        hidden[:, at] = (gate * jax.nn.sigmoid(gate) * up).astype(BF16)

    for copy in x_copies:
        copy.wait_send()
    own[2].wait()
    arrive(down_near)

    def group_start(g):
        if p.groups == 1:
            return 0
        return lax.rem(chip + g, chips) * p.columns

    def project(g):
        start = group_start(g)

        @pl.loop(0, p.columns // TILE)
        def _(t):
            at = pl.ds(aligned(start + t * TILE, LANES), TILE)
            a_send[:, at] = mul_t(hidden[...], down_w[at, :]).astype(BF16)

        return spread(a_send, y_home, main, pl.ds(aligned(start, LANES), p.columns))

    def project_chunk(k, chunk):
        begin, size = p.chunks[chunk]
        copies = []
        for side in range(2):
            owner = lax.rem(chip + chips - k, chips) * 2 + side
            at = pl.ds(aligned(owner * p.shard + begin, LANES), size)
            a_send[:, at] = mul_t(hidden[...], down_w[at, :]).astype(BF16)
            copies += spread(a_send, y_home, main, at)
        return copies

    def back(g):
        at_rows = pl.ds(aligned(group_start(g), LANES), p.columns)

        @pl.loop(0, p.hidden // TILE)
        def _(t):
            at = pl.ds(aligned(t * TILE, TILE), TILE)
            part = mul(c_in[:, at_rows], down_w[at_rows, at])
            if g == 0:
                hidden_cot[:, at] = part
            else:
                hidden_cot[:, at] += part

    def cot_arrives():
        arrive(c_copies)
        unpack(c_ext, c_in)
        fold_c[...] = mul_t(table[...], c_in[...])

    if p.groups > 1:
        y_copies = project(0)
        cot_arrives()
        back(0)
        for chunk in range(CHUNKS):
            arrive(forward(down_w, chunk, down_far[chunk]))
            for k in range(1, chips):
                y_copies += project_chunk(k, chunk)
    else:
        cot_arrives()
        for chunk in range(CHUNKS):
            arrive(forward(down_w, chunk, down_far[chunk]))
        y_copies = project(0)
        back(0)
    pack(a_send, a_ext)
    y_copies += spread(a_ext, y_ext, 16)
    for g in range(1, p.groups):
        back(g)

    @pl.loop(0, p.hidden // TILE)
    def _(t):
        at = pl.ds(aligned(t * TILE, TILE), TILE)
        gate, cot = gate_pre[:, at], hidden_cot[:, at]
        sig = jax.nn.sigmoid(gate)
        gate_cot[:, at] = (cot * up_pre[:, at] * sig * (1.0 + gate * (1.0 - sig))).astype(BF16)
        up_cot[:, at] = (cot * gate * sig).astype(BF16)

    for copy in c_copies:
        copy.wait_send()
    half = p.width // 2
    g_halves = []
    for h in range(2):

        @pl.loop(0, half // TILE)
        def _(t):
            at = pl.ds(aligned(h * half + t * TILE, TILE), TILE)
            b_send[:, at] = (
                mul_t(gate_cot[...], gate_w[at, :]) + mul_t(up_cot[...], up_w[at, :])
            ).astype(BF16)

        g_halves.append(spread(b_send, g_home, main, pl.ds(h * half, half)))
    pack(b_send, b_ext)
    g_rest = spread(b_ext, g_ext, 16)
    keep(a_send, y_home, main)
    keep(a_ext, y_ext, 16)
    keep(b_send, g_home, main)
    keep(b_ext, g_ext, 16)

    error_copy.wait()
    for m, (fold, right) in enumerate(((fold_x, gate_cot), (fold_x, up_cot), (fold_c, hidden))):
        high = fold[...].astype(BF16)
        low = (fold[...] - high.astype(F32)).astype(BF16)
        sketched = mul(high, right[...]) + mul(low, right[...])
        scaled = sketched * (4.0 / p.tokens) + sent[m]
        threshold = jnp.sum(jnp.abs(scaled)) / (SKETCH * p.hidden)
        kept = jnp.clip(scaled, -threshold, threshold)
        kept_out[0, 0, m] = kept
        sent[m] = scaled - kept
    mid = p.hidden // 2
    mine = pl.ds(aligned(core * mid, mid), mid)
    theirs = pl.ds(aligned((1 - core) * mid, mid), mid)
    pair_copy = remote(sent.at[:, :, theirs], pair, sibling)
    pair_copy.wait_recv()
    chip_sums[chip] = sent[:, :, mine] + pair[...]
    chip_copies = [
        remote(chip_sums.at[chip], chip_sums.at[chip], twin(k)) for k in range(1, chips)
    ]

    arrive(y_copies)
    lane_main = lax.broadcasted_iota(jnp.int32, (count, p.main_rows), 1)
    lane_ext = lax.broadcasted_iota(jnp.int32, (count, p.ext_rows), 1)
    home_main = [lane_main == main_index(*down_rows[k]) for k in range(2)]
    for i in range(p.pieces):
        value = 0.0
        for k in range(2):
            hit = lane_ext == ext_index(*down_rows[k], i)
            picked = mul(as_bf16(home_main[k]), y_home[:, piece_of(i)])
            picked += mul(as_bf16(hit), y_ext[...])
            value += weights[k] * picked
        layer_out[:, piece_of(i)] = value.astype(BF16)

    for copy in chip_copies:
        copy.wait_recv()
    pair_copy.wait_send()
    sent[:, :, mine] = functools.reduce(lambda a, b: a + b, [chip_sums[i] for i in range(chips)])
    total_copy = remote(sent.at[:, :, mine], total_half, sibling)
    results = [
        pltpu.make_async_copy(sent.at[:, :, mine], total_out.at[0, :, :, mine], local_sems.at[0])
    ]
    results[0].start()

    both_main = as_bf16(home_main[0] | home_main[1])
    arrive(g_rest)
    arrive(g_halves[0])
    for i in range(p.pieces):
        if i * 2 == p.pieces:
            arrive(g_halves[1])
        hit = (lane_ext == ext_index(*down_rows[0], i)) | (
            lane_ext == ext_index(*down_rows[1], i)
        )
        value = mul(both_main, g_home[:, piece_of(i)]) + mul(as_bf16(hit), g_ext[...])
        input_grad[:, piece_of(i)] = value.astype(BF16)

    total_copy.wait_recv()
    total_copy.wait_send()
    results.append(
        pltpu.make_async_copy(total_half, total_out.at[0, :, :, theirs], local_sems.at[1])
    )
    results[1].start()
    waited = {id(c) for c in x_copies + c_copies}
    for copy in outgoing + chip_copies:
        if id(copy) not in waited:
            copy.wait_send()
    for result in results:
        result.wait()


def on_device(
    experts,
    replicas,
    tokens,
    cotangent,
    routes,
    combine_weights,
    gate_weight,
    up_weight,
    down_weight_t,
    sketch_bucket,
    sketch_sign,
    error_state,
):
    count, width = tokens.shape
    units = gate_weight.shape[2]
    p = Plan(experts, replicas, count, width, units)
    vmem = pl.BlockSpec(memory_space=pltpu.VMEM)
    hbm = pl.BlockSpec(memory_space=pl.ANY)
    stage = (3, SKETCH, units)
    return pl.pallas_call(
        functools.partial(kernel, p),
        out_shape=(
            jax.ShapeDtypeStruct((count, width), BF16),
            jax.ShapeDtypeStruct((count, width), BF16),
            jax.ShapeDtypeStruct((1,) + stage, F32),
            jax.ShapeDtypeStruct((1, 1) + stage, F32),
        ),
        in_specs=[vmem] * 4 + [hbm] * 3 + [vmem] * 2 + [hbm],
        out_specs=(vmem, vmem, hbm, vmem),
        scratch_shapes=[pltpu.VMEM((width, units), BF16)] * 3
        + [pltpu.VMEM((p.rows, width), BF16)] * 4
        + [pltpu.VMEM((p.ext_rows, p.piece), BF16)] * 4
        + [pltpu.VMEM((p.main_rows, width), BF16)] * 2
        + [pltpu.VMEM((p.ext_rows, p.piece), BF16)] * 2
        + [pltpu.VMEM((p.rows, units), F32)] * 3
        + [pltpu.VMEM((p.rows, units), BF16)] * 3
        + [pltpu.VMEM((SKETCH, width), BF16)]
        + [pltpu.VMEM((SKETCH, p.rows), F32)] * 2
        + [
            pltpu.VMEM(stage, F32),
            pltpu.VMEM((3, SKETCH, units // 2), F32),
            pltpu.VMEM((p.chips, 3, SKETCH, units // 2), F32),
            pltpu.VMEM((3, SKETCH, units // 2), F32),
            pltpu.SemaphoreType.DMA((p.copies,)),
            pltpu.SemaphoreType.DMA((p.copies,)),
            pltpu.SemaphoreType.DMA((4,)),
        ],
        compiler_params=pltpu.CompilerParams(
            collective_id=0, has_side_effects=True, vmem_limit_bytes=63 * 2**20
        ),
    )(
        tokens,
        cotangent,
        routes.T,
        combine_weights.T,
        gate_weight,
        up_weight,
        down_weight_t,
        sketch_bucket.reshape(width // LANES, LANES),
        sketch_sign.reshape(width // LANES, LANES),
        error_state,
    )


def solution(mesh):
    in_specs = (
        P(("expert", "dp"), None),
        P(("expert", "dp"), None),
        P(("expert", "dp"), None),
        P(("expert", "dp"), None),
        P("expert", "dp", None),
        P("expert", "dp", None),
        P("expert", "dp", None),
        P(),
        P(),
        P("expert", "dp", None, None, None),
    )
    out_specs = (
        P(("expert", "dp"), None),
        P(("expert", "dp"), None),
        P("expert", None, None, None),
        P("expert", "dp", None, None, None),
    )
    body = functools.partial(on_device, mesh.shape["expert"], mesh.shape["dp"])
    return jax.shard_map(body, mesh=mesh, in_specs=in_specs, out_specs=out_specs, check_vma=False)
```
